32 devices in a mesh: row: 8 (over z, y), col: 4 (over x, core).
Axes of the slice: x: 2, y: 2, z: 4, core: 2. Of those that a mesh axis runs over, the one named last changes fastest.
Arguments:
- token_acts: bfloat16 [4, 1024, 768], P('col', 'row'), may hold values from -6 to 6
- pair_feats: bfloat16 [1024, 1024, 128], P('row', 'col'), may hold values from -6 to 6
- pair_mask: int32 [1024, 1024], P('row', 'col'), may hold values 0 or 1
- norm_gain: float32 [768], replicated, may hold values from 0.1 to 1.9
- norm_shift: float32 [768], replicated, may hold values from -3 to 3
- w_query: bfloat16 [768, 768], replicated, may hold values from -0.21875 to 0.21875
- query_bias: float32 [768], replicated, may hold values from -3 to 3
- w_key: bfloat16 [768, 768], replicated, may hold values from -0.21875 to 0.21875
- w_value: bfloat16 [768, 768], replicated, may hold values from -0.21875 to 0.21875
- w_gate: bfloat16 [768, 768], replicated, may hold values from -0.21875 to 0.21875
- w_out: bfloat16 [768, 768], replicated, may hold values from -0.21875 to 0.21875
- pair_gain: float32 [128], replicated, may hold values from 0.1 to 1.9
- w_pair: bfloat16 [128, 16], replicated, may hold values from -16 to 16, as said below
- grad_out: bfloat16 [4, 1024, 768], P('col', 'row'), may hold values from -6 to 6
Outputs:
- block_out: bfloat16 [4, 1024, 768], P('col', 'row')
- grad_acts: bfloat16 [4, 1024, 768], P('col', 'row')
- grad_pair: bfloat16 [1024, 1024, 128], P('row', 'col')
The draws below stay inside these ranges and needn't reach their ends.
Inputs may be any that keep to these rules, and one draw needn't show every extreme that they name: `w_pair`: entries of either sign.
All inputs are finite; a program needn't handle non-finite values. No bound on the sum of `pair_mask` on one device may be relied on, other than what follows from the above.
Results may differ from the reference program's by a relative error of at most 0.011.
The reference program's roundings to bfloat16 on the way count: a program that leaves them out, or rounds other values in their place, can miss the bound.
Values may be sent and summed in bfloat16 or wider, within the bound.
A program may use at most 192 MiB of HBM per device.

```python
import math
import jax
import jax.numpy as jnp
from jax import lax

D = 768
H = 16
C = 128
TR = 128
N = 1024
S = 4


def draw_w_pair(key, part):
    key = jax.random.fold_in(key, 11)
    base_key = jax.random.fold_in(key, 0)
    base_vals = jnp.clip(jax.random.normal(base_key, (C, H), jnp.float32), -3.0, 3.0)
    return (base_vals * (2.0 / math.sqrt(C))).astype(jnp.bfloat16)


def with_ends(drawn, rng, least, top_value):
    place = [jax.random.randint(jax.random.fold_in(rng, axis), (), 0, length) for axis, length in enumerate(drawn.shape)]
    longest = drawn.shape.index(max(drawn.shape))
    beside = place[:longest] + [(place[longest] + 1) % drawn.shape[longest]] + place[longest + 1:]
    return drawn.at[tuple(place)].set(least).at[tuple(beside)].set(top_value)


def shard_levels(stream_key, shape, cuts, least, top_value):
    gain, own = 1.0, jax.random.fold_in(stream_key, 6)
    for axis_at, parts in cuts:
        draws = jnp.exp(jax.random.uniform(jax.random.fold_in(own, axis_at), (parts,), jnp.float32, least / len(cuts), top_value / len(cuts)))
        gain = gain * jnp.repeat(draws, shape[axis_at] // parts).reshape([-1 if axis == axis_at else 1 for axis in range(len(shape))])
    return gain


def normal_values(key, extent, spread, limit, cuts=(), held_as=jnp.bfloat16):
    gain = shard_levels(key, extent, cuts, -0.22, 0.18) if cuts else 1.0
    result = jax.random.normal(key, extent, jnp.float32) * spread * gain
    return jnp.minimum(jnp.maximum(result, -limit), limit).astype(held_as)


def setup_inputs(seed: int = 0) -> dict:
    keys = jax.random.split(jax.random.key(seed), 15)
    token_acts = normal_values(keys[0], (S, N, D), 1.0, 6.0, ((0, 4), (1, 8)))
    pair_feats = normal_values(keys[1], (N, N, C), 1.0, 6.0, ((0, 8), (1, 4)))
    pair_mask = with_ends((jax.random.randint(keys[2], (N, N), 0, 4) < 3).astype(jnp.int32), jax.random.fold_in(keys[2], 1), 0, 1)
    norm_gain = jnp.clip(1.0 + 0.18 * jax.random.normal(keys[3], (D,), jnp.float32), 0.1, 1.9)
    norm_shift = normal_values(keys[4], (D,), 0.5, 3.0, (), jnp.float32)
    w_query = normal_values(keys[5], (D, D), D ** -0.5, 0.21875)
    query_bias = normal_values(keys[6], (D,), 0.5, 3.0, (), jnp.float32)
    w_key = normal_values(keys[7], (D, D), D ** -0.5, 0.21875)
    w_value = normal_values(keys[8], (D, D), D ** -0.5, 0.21875)
    w_gate = normal_values(keys[9], (D, D), D ** -0.5, 0.21875)
    w_out = normal_values(keys[10], (D, D), D ** -0.5, 0.21875)
    pair_gain = jnp.clip(1.0 + 0.18 * jax.random.normal(keys[11], (C,), jnp.float32), 0.1, 1.9)
    w_pair = draw_w_pair(jax.random.fold_in(keys[14], 71), 0)
    grad_out = normal_values(keys[13], (S, N, D), 1.0, 6.0, ((0, 4), (1, 8)))
    return dict(token_acts=token_acts, pair_feats=pair_feats, pair_mask=pair_mask, norm_gain=norm_gain, norm_shift=norm_shift, w_query=w_query, query_bias=query_bias, w_key=w_key, w_value=w_value, w_gate=w_gate, w_out=w_out, pair_gain=pair_gain, w_pair=w_pair, grad_out=grad_out)


epsilon = 1e-05
highest = lax.Precision.HIGHEST

def normalize(inputs):
    row_mean = lax.optimization_barrier(jnp.mean(inputs, axis=-1, keepdims=True))
    centred = inputs - row_mean
    variance = lax.optimization_barrier(jnp.mean(centred * centred, axis=-1, keepdims=True))
    inv_std = lax.rsqrt(variance + epsilon)
    return (centred * inv_std, inv_std)

def norm_backward(standard, inv_std, gain_vec, upstream):
    scaled = upstream * gain_vec
    grad_mean = lax.optimization_barrier(jnp.mean(scaled, axis=-1, keepdims=True))
    cross_mean = lax.optimization_barrier(jnp.mean(scaled * standard, axis=-1, keepdims=True))
    return (scaled - grad_mean - standard * cross_mean) * inv_std

def reference(token_acts, pair_feats, pair_mask, norm_gain, norm_shift, w_query, query_bias, w_key, w_value, w_gate, w_out, pair_gain, w_pair, grad_out):
    head_size = D // H
    score_scale = 1.0 / math.sqrt(head_size)
    block_ids = jnp.arange(N // TR, dtype=jnp.int32)
    pair_weight = w_pair.astype(jnp.float32)

    def bias_block(block_idx):
        start_row = (block_idx * TR).astype(jnp.int32)
        feats = lax.dynamic_slice_in_dim(pair_feats, start_row, TR, 0).astype(jnp.float32)
        standard, inv_std = normalize(feats)
        pnormed = lax.optimization_barrier((standard * pair_gain).astype(jnp.bfloat16))
        pair_bias = jnp.einsum('ijc,ch->hij', pnormed.astype(jnp.float32), pair_weight)
        mask_rows = lax.dynamic_slice_in_dim(pair_mask, start_row, TR, 0)
        row_index = start_row + lax.broadcasted_iota(jnp.int32, (TR, N), 0)
        col_index = lax.broadcasted_iota(jnp.int32, (TR, N), 1)
        allowed = (mask_rows == 1) | (row_index == col_index)
        return jnp.where(allowed[None], pair_bias, -1000000000.0).astype(jnp.bfloat16)
    biased = jnp.transpose(lax.map(bias_block, block_ids), (1, 0, 2, 3)).reshape(H, N, N)

    def sample_step(bias_grad, inputs):
        sample_act, sample_grad = inputs
        standard, inv_std = normalize(sample_act.astype(jnp.float32))
        normed = (standard * norm_gain + norm_shift).astype(jnp.bfloat16)
        query = (jnp.dot(normed, w_query, preferred_element_type=jnp.float32) + query_bias).astype(jnp.bfloat16)
        all_keys = jnp.dot(normed, w_key, preferred_element_type=jnp.float32).astype(jnp.bfloat16)
        all_values = jnp.dot(normed, w_value, preferred_element_type=jnp.float32).astype(jnp.bfloat16)
        gate_open = jax.nn.sigmoid(jnp.dot(normed, w_gate, preferred_element_type=jnp.float32))
        query_heads = query.reshape(N, H, head_size).astype(jnp.float32)
        key_heads = all_keys.reshape(N, H, head_size).astype(jnp.float32)
        value_heads = all_values.reshape(N, H, head_size).astype(jnp.float32)
        scores = jnp.einsum('ihe,jhe->hij', query_heads, key_heads) * score_scale + biased.astype(jnp.float32)
        attn_probs = jax.nn.softmax(scores, axis=-1)
        probs_b = lax.optimization_barrier(attn_probs.astype(jnp.bfloat16)).astype(jnp.float32)
        attended = jnp.einsum('hij,jhe->ihe', probs_b, value_heads).reshape(N, D)
        gated_out = (gate_open * attended).astype(jnp.bfloat16)
        sample_out = jnp.dot(gated_out, w_out, preferred_element_type=jnp.float32).astype(jnp.bfloat16)
        d_gated = jnp.einsum('io,do->id', sample_grad.astype(jnp.float32), w_out.astype(jnp.float32))
        d_att = lax.optimization_barrier((d_gated * gate_open).astype(jnp.bfloat16))
        d_gate_pre = d_gated * attended * gate_open * (1.0 - gate_open)
        att_heads = d_att.reshape(N, H, head_size).astype(jnp.float32)
        d_probs = jnp.einsum('ihe,jhe->hij', att_heads, value_heads)
        row_delta = lax.optimization_barrier(jnp.sum(attn_probs * d_probs, axis=-1, keepdims=True))
        d_scores = attn_probs * (d_probs - row_delta)
        ds_b = lax.optimization_barrier(d_scores.astype(jnp.bfloat16)).astype(jnp.float32)
        d_query = (jnp.einsum('hij,jhe->ihe', ds_b, key_heads) * score_scale).reshape(N, D)
        d_keys = (jnp.einsum('hij,ihe->jhe', ds_b, query_heads) * score_scale).reshape(N, D)
        d_values = jnp.einsum('hij,ihe->jhe', probs_b, att_heads).reshape(N, D)

        def back_project(upstream, matrix):
            return jnp.einsum('io,do->id', upstream, matrix.astype(jnp.float32), precision=highest)
        d_normed = back_project(d_query, w_query) + back_project(d_keys, w_key) + back_project(d_values, w_value) + back_project(d_gate_pre, w_gate)
        sample_dact = norm_backward(standard, inv_std, norm_gain, d_normed).astype(jnp.bfloat16)
        return (bias_grad + ds_b, (sample_out, sample_dact))
    bias_grad, (block_out, grad_acts) = lax.scan(sample_step, jnp.zeros((H, N, N), jnp.float32), (token_acts, grad_out))

    def pair_block(block_idx):
        start_row = (block_idx * TR).astype(jnp.int32)
        feats = lax.dynamic_slice_in_dim(pair_feats, start_row, TR, 0).astype(jnp.float32)
        standard, inv_std = normalize(feats)
        grad_rows = lax.dynamic_slice_in_dim(bias_grad, start_row, TR, 1)
        d_pnorm = jnp.einsum('hij,ch->ijc', grad_rows, pair_weight, precision=highest)
        return norm_backward(standard, inv_std, pair_gain, d_pnorm).astype(jnp.bfloat16)
    grad_pair = lax.map(pair_block, block_ids).reshape(N, N, C)
    return (block_out, grad_acts, grad_pair)
```

```python
import functools
import math

import jax
import jax.numpy as jnp
from jax import lax
from jax.experimental import pallas as pl
from jax.experimental.pallas import tpu as pltpu
from jax.sharding import PartitionSpec as P

epsilon = 1e-05
highest = lax.Precision.HIGHEST


def normalize(inputs):
    row_mean = jnp.mean(inputs, axis=-1, keepdims=True)
    centred = inputs - row_mean
    variance = jnp.mean(centred * centred, axis=-1, keepdims=True)
    inv_std = lax.rsqrt(variance + epsilon)
    return (centred * inv_std, inv_std)


def norm_backward(standard, inv_std, gain_vec, upstream):
    scaled = upstream * gain_vec
    grad_mean = jnp.mean(scaled, axis=-1, keepdims=True)
    cross_mean = jnp.mean(scaled * standard, axis=-1, keepdims=True)
    return (scaled - grad_mean - standard * cross_mean) * inv_std


def back_project(upstream, matrix):
    return jnp.einsum("io,do->id", upstream, matrix.astype(jnp.float32), precision=highest)


def place():
    row, col = lax.axis_index("row"), lax.axis_index("col")
    return row // 2, row % 2, col // 2, col % 2


def peer(line=None, side=None, chip=None, core=None):
    own = place()
    line, side, chip, core = (
        mine if given is None else given for mine, given in zip(own, (line, side, chip, core))
    )
    return (line * 2 + side, chip * 2 + core)


def remote(source, target, send_sem, recv_sem, device):
    return pltpu.make_async_remote_copy(
        src_ref=source,
        dst_ref=target,
        send_sem=send_sem,
        recv_sem=recv_sem,
        device_id=device,
        device_id_type=pl.DeviceIdType.MESH,
    )


def greet(lines, chips):
    line, side, chip, core = place()
    barrier = pltpu.get_barrier_semaphore()
    others = [peer(side=1 - side), peer(core=1 - core)]
    others += [peer(line=(line + 1) % lines), peer(line=(line + lines - 1) % lines)]
    others += [peer(chip=(chip + step) % chips) for step in range(1, chips)]
    for other in others:
        pl.semaphore_signal(barrier, inc=1, device_id=other, device_id_type=pl.DeviceIdType.MESH)
    pl.semaphore_wait(barrier, len(others))


def gather_kernel(
    lines, chips, kv, tile, kv_all, bias_all,
    local_sem, up_send, down_send, side_send, line_recv, side_recv,
    chip_send, chip_recv, core_send, core_recv,
):
    line, side, chip, core = place()
    width = tile.shape[2]
    greet(lines, chips)

    def slot(which_line, which_side):
        return kv_all.at[which_line * 2 + which_side]

    def columns(which_chip, which_core):
        start = pl.multiple_of((which_chip * 2 + which_core) * width, width)
        return bias_all.at[:, :, pl.ds(start, width)]

    sends = []
    for step in range(1, chips):
        sends.append(remote(
            tile, columns(chip, core), chip_send.at[step], chip_recv.at[step],
            peer(chip=(chip + step) % chips),
        ))
    sends.append(remote(
        tile, columns(chip, core), core_send.at[0], core_recv.at[0], peer(core=1 - core)
    ))
    for copy in sends:
        copy.start()

    def upward(source, origin):
        return remote(
            source, slot(origin, side), up_send.at[origin], line_recv.at[origin],
            peer(line=jnp.minimum(line + 1, lines - 1)),
        )

    def downward(source, origin):
        return remote(
            source, slot(origin, side), down_send.at[origin], line_recv.at[origin],
            peer(line=jnp.maximum(line - 1, 0)),
        )

    def sideward(source, origin):
        return remote(
            source, slot(origin, side), side_send.at[origin], side_recv.at[origin],
            peer(side=1 - side),
        )

    @pl.when(line < lines - 1)
    def _():
        upward(kv, line).start()

    @pl.when(line > 0)
    def _():
        downward(kv, line).start()

    sideward(kv, line).start()
    keep_kv = pltpu.make_async_copy(kv, slot(line, side), local_sem.at[0])
    keep_tile = pltpu.make_async_copy(tile, columns(chip, core), local_sem.at[1])
    keep_kv.start()
    keep_tile.start()

    for step in range(1, lines):
        @pl.when(line - step >= 0)
        def _():
            origin = line - step
            upward(slot(origin, side), origin).wait_recv()

            @pl.when(line < lines - 1)
            def _():
                upward(slot(origin, side), origin).start()

            sideward(slot(origin, side), origin).start()

        @pl.when(line + step < lines)
        def _():
            origin = line + step
            downward(slot(origin, side), origin).wait_recv()

            @pl.when(line > 0)
            def _():
                downward(slot(origin, side), origin).start()

            sideward(slot(origin, side), origin).start()

    for step in range(1, chips):
        origin = (chip + chips - step) % chips
        block = columns(origin, core)
        remote(tile, block, chip_send.at[step], chip_recv.at[step], peer(core=1 - core)).wait_recv()
        copy = remote(block, block, core_send.at[step], core_recv.at[step], peer(core=1 - core))
        copy.start()
        sends.append(copy)
    for step in range(chips):
        origin = (chip + chips - step) % chips
        block = columns(origin, 1 - core)
        remote(tile, block, core_send.at[step], core_recv.at[step], peer(core=1 - core)).wait_recv()
    for origin in range(lines):
        block = slot(origin, 1 - side)
        remote(
            kv, block, side_send.at[origin], side_recv.at[origin], peer(side=1 - side)
        ).wait_recv()
    for copy in sends:
        copy.wait_send()
    for origin in range(lines):
        sideward(kv, origin).wait_send()

        @pl.when((line < lines - 1) & (origin <= line))
        def _():
            upward(kv, origin).wait_send()

        @pl.when((line > 0) & (origin >= line))
        def _():
            downward(kv, origin).wait_send()

    keep_kv.wait()
    keep_tile.wait()


def gather(kv, tile, rows, cols):
    lines, chips = rows // 2, cols // 2
    heads, height, width = tile.shape
    anywhere = pl.BlockSpec(memory_space=pl.ANY)
    dma = pltpu.SemaphoreType.DMA
    return pl.pallas_call(
        functools.partial(gather_kernel, lines, chips),
        out_shape=(
            jax.ShapeDtypeStruct((rows,) + kv.shape, kv.dtype),
            jax.ShapeDtypeStruct((heads, height, width * cols), tile.dtype),
        ),
        in_specs=[anywhere] * 2,
        out_specs=(anywhere, anywhere),
        scratch_shapes=[
            dma((2,)), dma((lines,)), dma((lines,)), dma((lines,)), dma((lines,)), dma((lines,)),
            dma((chips,)), dma((chips,)), dma((chips,)), dma((chips,)),
        ],
        compiler_params=pltpu.CompilerParams(
            collective_id=0, has_side_effects=True, vmem_limit_bytes=48 * 2**20
        ),
    )(kv, tile)


def reduce_kernel(
    lines, chips, dkv, ds, kv_sum, ds_sum,
    side_in, line_out, up_in, down_in, core_in, chip_out, chip_in,
    side_send, side_recv, line_send, up_recv, down_recv,
    core_send, core_recv, chip_send, chip_recv,
):
    line, side, chip, core = place()
    heads, height, width = ds_sum.shape
    depth = kv_sum.shape[0]
    greet(lines, chips)

    def columns(which_chip, which_core):
        start = pl.multiple_of((which_chip * 2 + which_core) * width, width)
        return pl.ds(start, width)

    sends = []
    for step in [*range(1, chips), 0]:
        copy = remote(
            ds.at[:, :, columns((chip + step) % chips, 1 - core)], core_in.at[step],
            core_send.at[step], core_recv.at[step], peer(core=1 - core),
        )
        copy.start()
        sends.append(copy)
    order = []
    for step in range(lines):
        for item in (lines - 1 - step, step):
            if item not in order:
                order.append(item)
    for item in order:
        copy = remote(
            dkv.at[item * 2 + 1 - side], side_in.at[item], side_send.at[item],
            side_recv.at[item], peer(side=1 - side),
        )
        copy.start()
        sends.append(copy)
    for step in range(1, chips):
        other = (chip + step) % chips
        sends[step - 1].wait_recv()

        @pl.loop(0, heads)
        def _(head):
            mine = ds[head, :, columns(other, core)].astype(jnp.float32)
            total = mine + core_in[step, head].astype(jnp.float32)
            chip_out[step, head] = total.astype(chip_out.dtype)

        copy = remote(
            chip_out.at[step], chip_in.at[step], chip_send.at[step], chip_recv.at[step],
            peer(chip=other),
        )
        copy.start()
        sends.append(copy)

    chunk = 16

    def pieces(write):
        @pl.loop(0, depth // chunk)
        def _(piece):
            write(pl.ds(pl.multiple_of(piece * chunk, chunk), chunk))

    def pair(target, part):
        mine = dkv[target * 2 + side, part, :].astype(jnp.float32)
        return mine + side_in[target, part, :].astype(jnp.float32)

    def side_wait(target):
        remote(
            dkv.at[0], side_in.at[target], side_send.at[target], side_recv.at[target],
            peer(side=1 - side),
        ).wait_recv()

    def upward(target):
        return remote(
            line_out.at[target], up_in.at[target], line_send.at[target], up_recv.at[target],
            peer(line=jnp.minimum(line + 1, lines - 1)),
        )

    def downward(target):
        return remote(
            line_out.at[target], down_in.at[target], line_send.at[target], down_recv.at[target],
            peer(line=jnp.maximum(line - 1, 0)),
        )

    def pass_on(target, make, arrived, first):
        side_wait(target)

        @pl.when(first)
        def _():
            def write(part):
                line_out[target, part, :] = pair(target, part).astype(line_out.dtype)

            pieces(write)

        @pl.when(jnp.logical_not(first))
        def _():
            make(target).wait_recv()

            def write(part):
                total = pair(target, part) + arrived[target, part, :].astype(jnp.float32)
                line_out[target, part, :] = total.astype(line_out.dtype)

            pieces(write)

        make(target).start()

    for step in range(lines - 1):
        top = lines - 1 - step

        @pl.when(line < top)
        def _():
            pass_on(top, upward, up_in, line == 0)

        @pl.when(line > step)
        def _():
            pass_on(step, downward, down_in, line == lines - 1)

    side_wait(line)

    def write_pair(part):
        kv_sum[part, :] = pair(line, part)

    pieces(write_pair)

    @pl.when(line > 0)
    def _():
        upward(line).wait_recv()

        def write(part):
            kv_sum[part, :] += up_in[line, part, :].astype(jnp.float32)

        pieces(write)

    @pl.when(line < lines - 1)
    def _():
        downward(line).wait_recv()

        def write(part):
            kv_sum[part, :] += down_in[line, part, :].astype(jnp.float32)

        pieces(write)

    sends[chips - 1].wait_recv()
    for step in range(1, chips):
        remote(
            chip_out.at[step], chip_in.at[step], chip_send.at[step], chip_recv.at[step],
            peer(core=1 - core),
        ).wait_recv()

    @pl.loop(0, heads)
    def _(head):
        total = ds[head, :, columns(chip, core)].astype(jnp.float32)
        total += core_in[0, head].astype(jnp.float32)
        for step in range(1, chips):
            total += chip_in[step, head].astype(jnp.float32)
        ds_sum[head] = total.astype(ds_sum.dtype)

    for copy in sends:
        copy.wait_send()
    for target in range(lines):
        @pl.when(line != target)
        def _():
            upward(target).wait_send()


def reduce(dkv, ds, rows, cols):
    lines, chips = rows // 2, cols // 2
    heads, height, width = ds.shape
    width //= cols
    depth, wide = dkv.shape[0] // rows, dkv.shape[1]
    inside = pl.BlockSpec(memory_space=pltpu.VMEM)
    dma = pltpu.SemaphoreType.DMA
    half = jnp.bfloat16
    return pl.pallas_call(
        functools.partial(reduce_kernel, lines, chips),
        out_shape=(
            jax.ShapeDtypeStruct((depth, wide), jnp.float32),
            jax.ShapeDtypeStruct((heads, height, width), jnp.float32),
        ),
        in_specs=[inside] * 2,
        out_specs=(inside, inside),
        scratch_shapes=[
            *[pltpu.VMEM((lines, depth, wide), half)] * 4,
            *[pltpu.VMEM((chips, heads, height, width), half)] * 3,
            *[dma((lines,))] * 5,
            *[dma((chips,))] * 4,
        ],
        compiler_params=pltpu.CompilerParams(
            collective_id=1, has_side_effects=True, vmem_limit_bytes=52 * 2**20
        ),
    )(dkv.reshape(rows, depth, wide), ds)


def body(
    rows,
    cols,
    token_acts,
    pair_feats,
    pair_mask,
    norm_gain,
    norm_shift,
    w_query,
    query_bias,
    w_key,
    w_value,
    w_gate,
    w_out,
    pair_gain,
    w_pair,
    grad_out,
):
    row_count = token_acts.shape[1]
    model_width = token_acts.shape[2]
    col_count = pair_feats.shape[1]
    head_count = w_pair.shape[1]
    head_size = model_width // head_count
    score_scale = 1.0 / math.sqrt(head_size)
    row_start = lax.axis_index("row") * row_count
    col_start = lax.axis_index("col") * col_count
    pair_std, pair_inv = normalize(pair_feats.astype(jnp.float32))
    pnormed = (pair_std * pair_gain).astype(jnp.bfloat16)
    pair_bias = jnp.einsum("ijc,ch->hij", pnormed, w_pair, preferred_element_type=jnp.float32)
    row_index = row_start + lax.broadcasted_iota(jnp.int32, (row_count, col_count), 0)
    col_index = col_start + lax.broadcasted_iota(jnp.int32, (row_count, col_count), 1)
    allowed = (pair_mask == 1) | (row_index == col_index)
    biased = jnp.where(allowed[None], pair_bias, -1000000000.0).astype(jnp.bfloat16)
    standard, inv_std = normalize(token_acts[0].astype(jnp.float32))
    normed = (standard * norm_gain + norm_shift).astype(jnp.bfloat16)
    query = (jnp.dot(normed, w_query, preferred_element_type=jnp.float32) + query_bias).astype(
        jnp.bfloat16
    )
    gate_open = jax.nn.sigmoid(jnp.dot(normed, w_gate, preferred_element_type=jnp.float32))
    own_keys = jnp.dot(normed, w_key, preferred_element_type=jnp.float32).astype(jnp.bfloat16)
    own_values = jnp.dot(normed, w_value, preferred_element_type=jnp.float32).astype(jnp.bfloat16)
    both, bias_full = gather(jnp.concatenate([own_keys, own_values], axis=1), biased, rows, cols)
    both = both.reshape(rows * row_count, 2 * model_width)
    all_keys, all_values = both[:, :model_width], both[:, model_width:]
    key_count = all_keys.shape[0]
    query_heads = query.reshape(row_count, head_count, head_size)
    key_heads = all_keys.reshape(key_count, head_count, head_size)
    value_heads = all_values.reshape(key_count, head_count, head_size)
    scores = jnp.einsum(
        "ihe,jhe->hij", query_heads, key_heads, preferred_element_type=jnp.float32
    ) * score_scale + bias_full.astype(jnp.float32)
    attn_probs = jax.nn.softmax(scores, axis=-1)
    probs_b = attn_probs.astype(jnp.bfloat16)
    attended = jnp.einsum(
        "hij,jhe->ihe", probs_b, value_heads, preferred_element_type=jnp.float32
    ).reshape(row_count, model_width)
    gated_out = (gate_open * attended).astype(jnp.bfloat16)
    block_out = jnp.dot(gated_out, w_out, preferred_element_type=jnp.float32).astype(jnp.bfloat16)
    d_gated = jnp.einsum("io,do->id", grad_out[0], w_out, preferred_element_type=jnp.float32)
    d_att = (d_gated * gate_open).astype(jnp.bfloat16)
    d_gate_pre = d_gated * attended * gate_open * (1.0 - gate_open)
    att_heads = d_att.reshape(row_count, head_count, head_size)
    d_probs = jnp.einsum("ihe,jhe->hij", att_heads, value_heads, preferred_element_type=jnp.float32)
    row_delta = jnp.sum(attn_probs * d_probs, axis=-1, keepdims=True)
    d_scores = attn_probs * (d_probs - row_delta)
    ds_b = d_scores.astype(jnp.bfloat16)
    d_query = (
        jnp.einsum("hij,jhe->ihe", ds_b, key_heads, preferred_element_type=jnp.float32)
        * score_scale
    ).reshape(row_count, model_width)
    d_keys = (
        jnp.einsum("hij,ihe->jhe", ds_b, query_heads, preferred_element_type=jnp.float32)
        * score_scale
    ).reshape(key_count, model_width)
    d_values = jnp.einsum(
        "hij,ihe->jhe", probs_b, att_heads, preferred_element_type=jnp.float32
    ).reshape(key_count, model_width)
    near_part = back_project(d_query, w_query) + back_project(d_gate_pre, w_gate)
    summed, bias_grad = reduce(
        jnp.concatenate([d_keys, d_values], axis=1).astype(jnp.bfloat16), ds_b, rows, cols
    )
    key_grad, value_grad = summed[:, :model_width], summed[:, model_width:]
    far_part = back_project(key_grad, w_key) + back_project(value_grad, w_value)
    d_normed = near_part + far_part
    grad_acts = norm_backward(standard, inv_std, norm_gain, d_normed).astype(jnp.bfloat16)
    d_pnorm = jnp.einsum("hij,ch->ijc", bias_grad, w_pair.astype(jnp.float32), precision=highest)
    grad_pair = norm_backward(pair_std, pair_inv, pair_gain, d_pnorm).astype(jnp.bfloat16)
    return (block_out[None], grad_acts[None], grad_pair)


def solution(mesh):
    placed = (
        P("col", "row", None),
        P("row", "col", None),
        P("row", "col"),
        P(),
        P(),
        P(),
        P(),
        P(),
        P(),
        P(),
        P(),
        P(),
        P(),
        P("col", "row", None),
    )
    return jax.shard_map(
        functools.partial(body, mesh.shape["row"], mesh.shape["col"]),
        mesh=mesh,
        in_specs=placed,
        out_specs=(P("col", "row", None), P("col", "row", None), P("row", "col", None)),
        check_vma=False,
    )
```

```python
import functools
import math

import jax
import jax.numpy as jnp
from jax import lax
from jax.experimental import pallas as pl
from jax.experimental.pallas import tpu as pltpu
from jax.sharding import PartitionSpec as P

epsilon = 1e-05
highest = lax.Precision.HIGHEST


def normalize(inputs):
    row_mean = jnp.mean(inputs, axis=-1, keepdims=True)
    centred = inputs - row_mean
    variance = jnp.mean(centred * centred, axis=-1, keepdims=True)
    inv_std = lax.rsqrt(variance + epsilon)
    return (centred * inv_std, inv_std)


def norm_backward(standard, inv_std, gain_vec, upstream):
    scaled = upstream * gain_vec
    grad_mean = jnp.mean(scaled, axis=-1, keepdims=True)
    cross_mean = jnp.mean(scaled * standard, axis=-1, keepdims=True)
    return (scaled - grad_mean - standard * cross_mean) * inv_std


def back_project(upstream, matrix):
    return jnp.einsum("io,do->id", upstream, matrix.astype(jnp.float32), precision=highest)


def place():
    row, col = lax.axis_index("row"), lax.axis_index("col")
    return row // 2, row % 2, col // 2, col % 2


def peer(line=None, side=None, chip=None, core=None):
    own = place()
    line, side, chip, core = (
        mine if given is None else given for mine, given in zip(own, (line, side, chip, core))
    )
    return (line * 2 + side, chip * 2 + core)


def remote(source, target, send_sem, recv_sem, device):
    return pltpu.make_async_remote_copy(
        src_ref=source,
        dst_ref=target,
        send_sem=send_sem,
        recv_sem=recv_sem,
        device_id=device,
        device_id_type=pl.DeviceIdType.MESH,
    )


def greet(lines, chips):
    line, side, chip, core = place()
    barrier = pltpu.get_barrier_semaphore()
    others = [peer(side=1 - side), peer(core=1 - core)]
    others += [peer(line=(line + 1) % lines), peer(line=(line + lines - 1) % lines)]
    others += [peer(chip=(chip + step) % chips) for step in range(1, chips)]
    for other in others:
        pl.semaphore_signal(barrier, inc=1, device_id=other, device_id_type=pl.DeviceIdType.MESH)
    pl.semaphore_wait(barrier, len(others))


def gather_kernel(
    lines, chips, kv, tile, kv_all, bias_all,
    local_sem, up_send, down_send, side_send, line_recv, side_recv,
    chip_send, chip_recv, core_send, core_recv,
):
    line, side, chip, core = place()
    width = tile.shape[2]
    greet(lines, chips)

    def slot(which_line, which_side):
        return kv_all.at[which_line * 2 + which_side]

    def columns(which_chip, which_core):
        start = pl.multiple_of((which_chip * 2 + which_core) * width, width)
        return bias_all.at[:, :, pl.ds(start, width)]

    sends = []
    for step in range(1, chips):
        sends.append(remote(
            tile, columns(chip, core), chip_send.at[step], chip_recv.at[step],
            peer(chip=(chip + step) % chips),
        ))
    sends.append(remote(
        tile, columns(chip, core), core_send.at[0], core_recv.at[0], peer(core=1 - core)
    ))
    for copy in sends:
        copy.start()

    def upward(source, origin):
        return remote(
            source, slot(origin, side), up_send.at[origin], line_recv.at[origin],
            peer(line=jnp.minimum(line + 1, lines - 1)),
        )

    def downward(source, origin):
        return remote(
            source, slot(origin, side), down_send.at[origin], line_recv.at[origin],
            peer(line=jnp.maximum(line - 1, 0)),
        )

    def sideward(source, origin):
        return remote(
            source, slot(origin, side), side_send.at[origin], side_recv.at[origin],
            peer(side=1 - side),
        )

    @pl.when(line < lines - 1)
    def _():
        upward(kv, line).start()

    @pl.when(line > 0)
    def _():
        downward(kv, line).start()

    sideward(kv, line).start()
    keep_kv = pltpu.make_async_copy(kv, slot(line, side), local_sem.at[0])
    keep_tile = pltpu.make_async_copy(tile, columns(chip, core), local_sem.at[1])
    keep_kv.start()
    keep_tile.start()

    for step in range(1, lines):
        @pl.when(line - step >= 0)
        def _():
            origin = line - step
            upward(slot(origin, side), origin).wait_recv()

            @pl.when(line < lines - 1)
            def _():
                upward(slot(origin, side), origin).start()

            sideward(slot(origin, side), origin).start()

        @pl.when(line + step < lines)
        def _():
            origin = line + step
            downward(slot(origin, side), origin).wait_recv()

            @pl.when(line > 0)
            def _():
                downward(slot(origin, side), origin).start()

            sideward(slot(origin, side), origin).start()

    for step in range(1, chips):
        origin = (chip + chips - step) % chips
        block = columns(origin, core)
        remote(tile, block, chip_send.at[step], chip_recv.at[step], peer(core=1 - core)).wait_recv()
        copy = remote(block, block, core_send.at[step], core_recv.at[step], peer(core=1 - core))
        copy.start()
        sends.append(copy)
    for step in range(chips):
        origin = (chip + chips - step) % chips
        block = columns(origin, 1 - core)
        remote(tile, block, core_send.at[step], core_recv.at[step], peer(core=1 - core)).wait_recv()
    for origin in range(lines):
        block = slot(origin, 1 - side)
        remote(
            kv, block, side_send.at[origin], side_recv.at[origin], peer(side=1 - side)
        ).wait_recv()
    for copy in sends:
        copy.wait_send()
    for origin in range(lines):
        sideward(kv, origin).wait_send()

        @pl.when((line < lines - 1) & (origin <= line))
        def _():
            upward(kv, origin).wait_send()

        @pl.when((line > 0) & (origin >= line))
        def _():
            downward(kv, origin).wait_send()

    keep_kv.wait()
    keep_tile.wait()


def gather(kv, tile, rows, cols):
    lines, chips = rows // 2, cols // 2
    heads, height, width = tile.shape
    anywhere = pl.BlockSpec(memory_space=pl.ANY)
    dma = pltpu.SemaphoreType.DMA
    return pl.pallas_call(
        functools.partial(gather_kernel, lines, chips),
        out_shape=(
            jax.ShapeDtypeStruct((rows,) + kv.shape, kv.dtype),
            jax.ShapeDtypeStruct((heads, height, width * cols), tile.dtype),
        ),
        in_specs=[anywhere] * 2,
        out_specs=(anywhere, anywhere),
        scratch_shapes=[
            dma((2,)), dma((lines,)), dma((lines,)), dma((lines,)), dma((lines,)), dma((lines,)),
            dma((chips,)), dma((chips,)), dma((chips,)), dma((chips,)),
        ],
        compiler_params=pltpu.CompilerParams(
            collective_id=0, has_side_effects=True, vmem_limit_bytes=48 * 2**20
        ),
    )(kv, tile)


def reduce_kernel(
    lines, chips, dkv, ds, kv_sum, ds_sum,
    side_in, line_out, up_in, down_in, core_in, chip_out, chip_in,
    side_send, side_recv, line_send, up_recv, down_recv,
    core_send, core_recv, chip_send, chip_recv,
):
    line, side, chip, core = place()
    heads, height, width = ds_sum.shape
    depth = kv_sum.shape[0]
    greet(lines, chips)

    def columns(which_chip, which_core):
        start = pl.multiple_of((which_chip * 2 + which_core) * width, width)
        return pl.ds(start, width)

    sends = []
    for step in [*range(1, chips), 0]:
        copy = remote(
            ds.at[:, :, columns((chip + step) % chips, 1 - core)], core_in.at[step],
            core_send.at[step], core_recv.at[step], peer(core=1 - core),
        )
        copy.start()
        sends.append(copy)
    order = []
    for step in range(lines):
        for item in (lines - 1 - step, step):
            if item not in order:
                order.append(item)
    for item in order:
        copy = remote(
            dkv.at[item * 2 + 1 - side], side_in.at[item], side_send.at[item],
            side_recv.at[item], peer(side=1 - side),
        )
        copy.start()
        sends.append(copy)
    for step in range(1, chips):
        other = (chip + step) % chips
        sends[step - 1].wait_recv()

        @pl.loop(0, heads)
        def _(head):
            mine = ds[head, :, columns(other, core)].astype(jnp.float32)
            total = mine + core_in[step, head].astype(jnp.float32)
            chip_out[step, head] = total.astype(chip_out.dtype)

        copy = remote(
            chip_out.at[step], chip_in.at[step], chip_send.at[step], chip_recv.at[step],
            peer(chip=other),
        )
        copy.start()
        sends.append(copy)

    chunk = 16

    def pieces(write):
        @pl.loop(0, depth // chunk)
        def _(piece):
            write(pl.ds(pl.multiple_of(piece * chunk, chunk), chunk))

    def pair(target, part):
        mine = dkv[target * 2 + side, part, :].astype(jnp.float32)
        return mine + side_in[target, part, :].astype(jnp.float32)

    def side_wait(target):
        remote(
            dkv.at[0], side_in.at[target], side_send.at[target], side_recv.at[target],
            peer(side=1 - side),
        ).wait_recv()

    def upward(target):
        return remote(
            line_out.at[target], up_in.at[target], line_send.at[target], up_recv.at[target],
            peer(line=jnp.minimum(line + 1, lines - 1)),
        )

    def downward(target):
        return remote(
            line_out.at[target], down_in.at[target], line_send.at[target], down_recv.at[target],
            peer(line=jnp.maximum(line - 1, 0)),
        )

    def pass_on(target, make, arrived, first):
        side_wait(target)

        @pl.when(first)
        def _():
            def write(part):
                line_out[target, part, :] = pair(target, part).astype(line_out.dtype)

            pieces(write)

        @pl.when(jnp.logical_not(first))
        def _():
            make(target).wait_recv()

            def write(part):
                total = pair(target, part) + arrived[target, part, :].astype(jnp.float32)
                line_out[target, part, :] = total.astype(line_out.dtype)

            pieces(write)

        make(target).start()

    for step in range(lines - 1):
        top = lines - 1 - step

        @pl.when(line < top)
        def _():
            pass_on(top, upward, up_in, line == 0)

        @pl.when(line > step)
        def _():
            pass_on(step, downward, down_in, line == lines - 1)

    side_wait(line)

    def write_pair(part):
        kv_sum[part, :] = pair(line, part)

    pieces(write_pair)

    @pl.when(line > 0)
    def _():
        upward(line).wait_recv()

        def write(part):
            kv_sum[part, :] += up_in[line, part, :].astype(jnp.float32)

        pieces(write)

    @pl.when(line < lines - 1)
    def _():
        downward(line).wait_recv()

        def write(part):
            kv_sum[part, :] += down_in[line, part, :].astype(jnp.float32)

        pieces(write)

    sends[chips - 1].wait_recv()
    for step in range(1, chips):
        remote(
            chip_out.at[step], chip_in.at[step], chip_send.at[step], chip_recv.at[step],
            peer(core=1 - core),
        ).wait_recv()

    @pl.loop(0, heads)
    def _(head):
        total = ds[head, :, columns(chip, core)].astype(jnp.float32)
        total += core_in[0, head].astype(jnp.float32)
        for step in range(1, chips):
            total += chip_in[step, head].astype(jnp.float32)
        ds_sum[head] = total.astype(ds_sum.dtype)

    for copy in sends:
        copy.wait_send()
    for target in range(lines):
        @pl.when(line != target)
        def _():
            upward(target).wait_send()


def reduce(dkv, ds, rows, cols):
    lines, chips = rows // 2, cols // 2
    heads, height, width = ds.shape
    width //= cols
    depth, wide = dkv.shape[0] // rows, dkv.shape[1]
    inside = pl.BlockSpec(memory_space=pltpu.VMEM)
    dma = pltpu.SemaphoreType.DMA
    half = jnp.bfloat16
    return pl.pallas_call(
        functools.partial(reduce_kernel, lines, chips),
        out_shape=(
            jax.ShapeDtypeStruct((depth, wide), jnp.float32),
            jax.ShapeDtypeStruct((heads, height, width), jnp.float32),
        ),
        in_specs=[inside] * 2,
        out_specs=(inside, inside),
        scratch_shapes=[
            *[pltpu.VMEM((lines, depth, wide), half)] * 4,
            *[pltpu.VMEM((chips, heads, height, width), half)] * 3,
            *[dma((lines,))] * 5,
            *[dma((chips,))] * 4,
        ],
        compiler_params=pltpu.CompilerParams(
            collective_id=1, has_side_effects=True, vmem_limit_bytes=52 * 2**20
        ),
    )(dkv.reshape(rows, depth, wide), ds)


def lane_mean(values, ones):
    high = values.astype(jnp.bfloat16)
    low = (values - high.astype(jnp.float32)).astype(jnp.bfloat16)
    return jnp.dot(
        jnp.concatenate([high, low], axis=1), ones, preferred_element_type=jnp.float32
    )


def pair_standard(feats, centre, ones):
    centred = jnp.dot(feats, centre, preferred_element_type=jnp.float32)
    inv_std = lax.rsqrt(lane_mean(centred * centred, ones) + epsilon)
    return centred * inv_std, inv_std


def pair_forward_kernel(feats, centre, ones, gain, weights, out):
    for item in range(feats.shape[0]):
        standard, _ = pair_standard(feats[item], centre[...], ones[...])
        normed = (standard * gain[...]).astype(jnp.bfloat16)
        out[item] = lax.dot_general(
            weights[...], normed, (((1,), (1,)), ((), ())), preferred_element_type=jnp.float32
        ).astype(jnp.bfloat16)


def pair_backward_kernel(feats, centre, ones, bias_grad, weights, out):
    for item in range(feats.shape[0]):
        standard, inv_std = pair_standard(feats[item], centre[...], ones[...])
        grad = bias_grad[item]
        high = grad.astype(jnp.bfloat16).astype(jnp.float32)
        low = grad - high
        parts = jnp.concatenate([high, low, high, low], axis=0).T.astype(jnp.bfloat16)
        scaled = jnp.dot(parts, weights[...], preferred_element_type=jnp.float32)
        cross_mean = lane_mean(scaled * standard, ones[...])
        out[item] = ((scaled - standard * cross_mean) * inv_std).astype(jnp.bfloat16)


def pair_call(kernel, pair_feats, extra, extra_specs, out_shape, block=8):
    rows, width, channels = pair_feats.shape
    eye = jnp.eye(channels, dtype=jnp.float32)
    centre = (eye - 1.0 / channels).astype(jnp.bfloat16)
    ones = jnp.full((2 * channels, channels), 1.0 / channels, jnp.bfloat16)
    whole = lambda shape: pl.BlockSpec(shape, lambda step: (0,) * len(shape))
    tiled = lambda shape: pl.BlockSpec((block,) + shape[1:], lambda step: (step, 0, 0))
    return pl.pallas_call(
        kernel,
        grid=(rows // block,),
        out_shape=jax.ShapeDtypeStruct(out_shape, jnp.bfloat16),
        in_specs=[
            tiled(pair_feats.shape), whole(centre.shape), whole(ones.shape),
            *[(tiled if spec else whole)(item.shape) for item, spec in zip(extra, extra_specs)],
        ],
        out_specs=tiled(out_shape),
        compiler_params=pltpu.CompilerParams(vmem_limit_bytes=32 * 2**20),
    )(pair_feats, centre, ones, *extra)


def pair_forward(pair_feats, pair_gain, w_pair):
    rows, width, channels = pair_feats.shape
    return pair_call(
        pair_forward_kernel, pair_feats, (pair_gain[None], w_pair.T), (False, False),
        (rows, w_pair.shape[1], width),
    )


def pair_backward(pair_feats, pair_gain, w_pair, bias_grad):
    scaled = w_pair.astype(jnp.float32).T * pair_gain
    scaled = scaled - jnp.mean(scaled, axis=1, keepdims=True)
    high = lax.reduce_precision(scaled, 8, 7)
    low = scaled - high
    weights = jnp.concatenate([high, high, low, low], axis=0).astype(jnp.bfloat16)
    return pair_call(
        pair_backward_kernel, pair_feats, (jnp.transpose(bias_grad, (1, 0, 2)), weights),
        (True, False), pair_feats.shape,
    )


def body(
    rows,
    cols,
    token_acts,
    pair_feats,
    pair_mask,
    norm_gain,
    norm_shift,
    w_query,
    query_bias,
    w_key,
    w_value,
    w_gate,
    w_out,
    pair_gain,
    w_pair,
    grad_out,
):
    row_count = token_acts.shape[1]
    model_width = token_acts.shape[2]
    col_count = pair_feats.shape[1]
    head_count = w_pair.shape[1]
    head_size = model_width // head_count
    score_scale = 1.0 / math.sqrt(head_size)
    row_start = lax.axis_index("row") * row_count
    col_start = lax.axis_index("col") * col_count
    pair_bias = jnp.transpose(pair_forward(pair_feats, pair_gain, w_pair), (1, 0, 2))
    row_index = row_start + lax.broadcasted_iota(jnp.int32, (row_count, col_count), 0)
    col_index = col_start + lax.broadcasted_iota(jnp.int32, (row_count, col_count), 1)
    allowed = (pair_mask == 1) | (row_index == col_index)
    biased = jnp.where(allowed[None], pair_bias, jnp.bfloat16(-1000000000.0))
    standard, inv_std = normalize(token_acts[0].astype(jnp.float32))
    normed = (standard * norm_gain + norm_shift).astype(jnp.bfloat16)
    query = (jnp.dot(normed, w_query, preferred_element_type=jnp.float32) + query_bias).astype(
        jnp.bfloat16
    )
    gate_open = jax.nn.sigmoid(jnp.dot(normed, w_gate, preferred_element_type=jnp.float32))
    own_keys = jnp.dot(normed, w_key, preferred_element_type=jnp.float32).astype(jnp.bfloat16)
    own_values = jnp.dot(normed, w_value, preferred_element_type=jnp.float32).astype(jnp.bfloat16)
    both, bias_full = gather(jnp.concatenate([own_keys, own_values], axis=1), biased, rows, cols)
    both = both.reshape(rows * row_count, 2 * model_width)
    all_keys, all_values = both[:, :model_width], both[:, model_width:]
    key_count = all_keys.shape[0]
    query_heads = query.reshape(row_count, head_count, head_size)
    key_heads = all_keys.reshape(key_count, head_count, head_size)
    value_heads = all_values.reshape(key_count, head_count, head_size)
    scores = jnp.einsum(
        "ihe,jhe->hij", query_heads, key_heads, preferred_element_type=jnp.float32
    ) * score_scale + bias_full.astype(jnp.float32)
    attn_probs = jax.nn.softmax(scores, axis=-1)
    probs_b = attn_probs.astype(jnp.bfloat16)
    attended = jnp.einsum(
        "hij,jhe->ihe", probs_b, value_heads, preferred_element_type=jnp.float32
    ).reshape(row_count, model_width)
    gated_out = (gate_open * attended).astype(jnp.bfloat16)
    block_out = jnp.dot(gated_out, w_out, preferred_element_type=jnp.float32).astype(jnp.bfloat16)
    d_gated = jnp.einsum("io,do->id", grad_out[0], w_out, preferred_element_type=jnp.float32)
    d_att = (d_gated * gate_open).astype(jnp.bfloat16)
    d_gate_pre = d_gated * attended * gate_open * (1.0 - gate_open)
    att_heads = d_att.reshape(row_count, head_count, head_size)
    d_probs = jnp.einsum("ihe,jhe->hij", att_heads, value_heads, preferred_element_type=jnp.float32)
    row_delta = jnp.sum(attn_probs * d_probs, axis=-1, keepdims=True)
    d_scores = attn_probs * (d_probs - row_delta)
    ds_b = d_scores.astype(jnp.bfloat16)
    d_query = (
        jnp.einsum("hij,jhe->ihe", ds_b, key_heads, preferred_element_type=jnp.float32)
        * score_scale
    ).reshape(row_count, model_width)
    d_keys = (
        jnp.einsum("hij,ihe->jhe", ds_b, query_heads, preferred_element_type=jnp.float32)
        * score_scale
    ).reshape(key_count, model_width)
    d_values = jnp.einsum(
        "hij,ihe->jhe", probs_b, att_heads, preferred_element_type=jnp.float32
    ).reshape(key_count, model_width)
    near_part = back_project(d_query, w_query) + back_project(d_gate_pre, w_gate)
    summed, bias_grad = reduce(
        jnp.concatenate([d_keys, d_values], axis=1).astype(jnp.bfloat16), ds_b, rows, cols
    )
    key_grad, value_grad = summed[:, :model_width], summed[:, model_width:]
    far_part = back_project(key_grad, w_key) + back_project(value_grad, w_value)
    d_normed = near_part + far_part
    grad_acts = norm_backward(standard, inv_std, norm_gain, d_normed).astype(jnp.bfloat16)
    grad_pair = pair_backward(pair_feats, pair_gain, w_pair, bias_grad)
    return (block_out[None], grad_acts[None], grad_pair)


def solution(mesh):
    placed = (
        P("col", "row", None),
        P("row", "col", None),
        P("row", "col"),
        P(),
        P(),
        P(),
        P(),
        P(),
        P(),
        P(),
        P(),
        P(),
        P(),
        P("col", "row", None),
    )
    return jax.shard_map(
        functools.partial(body, mesh.shape["row"], mesh.shape["col"]),
        mesh=mesh,
        in_specs=placed,
        out_specs=(P("col", "row", None), P("col", "row", None), P("row", "col", None)),
        check_vma=False,
    )
```

```python
import functools
import math

import jax
import jax.numpy as jnp
from jax import lax
from jax.experimental import pallas as pl
from jax.experimental.pallas import tpu as pltpu
from jax.sharding import PartitionSpec as P

epsilon = 1e-05
highest = lax.Precision.HIGHEST


def normalize(inputs):
    row_mean = jnp.mean(inputs, axis=-1, keepdims=True)
    centred = inputs - row_mean
    variance = jnp.mean(centred * centred, axis=-1, keepdims=True)
    inv_std = lax.rsqrt(variance + epsilon)
    return (centred * inv_std, inv_std)


def norm_backward(standard, inv_std, gain_vec, upstream):
    scaled = upstream * gain_vec
    grad_mean = jnp.mean(scaled, axis=-1, keepdims=True)
    cross_mean = jnp.mean(scaled * standard, axis=-1, keepdims=True)
    return (scaled - grad_mean - standard * cross_mean) * inv_std


def back_project(upstream, matrix):
    return jnp.einsum("io,do->id", upstream, matrix.astype(jnp.float32), precision=highest)


def place():
    row, col = lax.axis_index("row"), lax.axis_index("col")
    return row // 2, row % 2, col // 2, col % 2


def peer(line=None, side=None, chip=None, core=None):
    own = place()
    line, side, chip, core = (
        mine if given is None else given for mine, given in zip(own, (line, side, chip, core))
    )
    return (line * 2 + side, chip * 2 + core)


def remote(source, target, send_sem, recv_sem, device):
    return pltpu.make_async_remote_copy(
        src_ref=source,
        dst_ref=target,
        send_sem=send_sem,
        recv_sem=recv_sem,
        device_id=device,
        device_id_type=pl.DeviceIdType.MESH,
    )


def greet(lines, chips):
    line, side, chip, core = place()
    barrier = pltpu.get_barrier_semaphore()
    others = [peer(side=1 - side), peer(core=1 - core)]
    others += [peer(line=(line + 1) % lines), peer(line=(line + lines - 1) % lines)]
    others += [peer(chip=(chip + step) % chips) for step in range(1, chips)]
    for other in others:
        pl.semaphore_signal(barrier, inc=1, device_id=other, device_id_type=pl.DeviceIdType.MESH)
    pl.semaphore_wait(barrier, len(others))


def gather_kernel(
    lines, chips, kv, tile, kv_all, bias_all,
    local_sem, up_send, down_send, side_send, line_recv, side_recv,
    chip_send, chip_recv, core_send, core_recv,
):
    line, side, chip, core = place()
    width = tile.shape[2]
    greet(lines, chips)

    def slot(which_line, which_side):
        return kv_all.at[which_line * 2 + which_side]

    def columns(which_chip, which_core):
        start = pl.multiple_of((which_chip * 2 + which_core) * width, width)
        return bias_all.at[:, :, pl.ds(start, width)]

    sends = []
    for step in range(1, chips):
        sends.append(remote(
            tile, columns(chip, core), chip_send.at[step], chip_recv.at[step],
            peer(chip=(chip + step) % chips),
        ))
    sends.append(remote(
        tile, columns(chip, core), core_send.at[0], core_recv.at[0], peer(core=1 - core)
    ))
    for copy in sends:
        copy.start()

    def upward(source, origin):
        return remote(
            source, slot(origin, side), up_send.at[origin], line_recv.at[origin],
            peer(line=jnp.minimum(line + 1, lines - 1)),
        )

    def downward(source, origin):
        return remote(
            source, slot(origin, side), down_send.at[origin], line_recv.at[origin],
            peer(line=jnp.maximum(line - 1, 0)),
        )

    def sideward(source, origin):
        return remote(
            source, slot(origin, side), side_send.at[origin], side_recv.at[origin],
            peer(side=1 - side),
        )

    @pl.when(line < lines - 1)
    def _():
        upward(kv, line).start()

    @pl.when(line > 0)
    def _():
        downward(kv, line).start()

    sideward(kv, line).start()
    keep_kv = pltpu.make_async_copy(kv, slot(line, side), local_sem.at[0])
    keep_tile = pltpu.make_async_copy(tile, columns(chip, core), local_sem.at[1])
    keep_kv.start()
    keep_tile.start()

    for step in range(1, lines):
        @pl.when(line - step >= 0)
        def _():
            origin = line - step
            upward(slot(origin, side), origin).wait_recv()

            @pl.when(line < lines - 1)
            def _():
                upward(slot(origin, side), origin).start()

            sideward(slot(origin, side), origin).start()

        @pl.when(line + step < lines)
        def _():
            origin = line + step
            downward(slot(origin, side), origin).wait_recv()

            @pl.when(line > 0)
            def _():
                downward(slot(origin, side), origin).start()

            sideward(slot(origin, side), origin).start()

    for step in range(1, chips):
        origin = (chip + chips - step) % chips
        block = columns(origin, core)
        remote(tile, block, chip_send.at[step], chip_recv.at[step], peer(core=1 - core)).wait_recv()
        copy = remote(block, block, core_send.at[step], core_recv.at[step], peer(core=1 - core))
        copy.start()
        sends.append(copy)
    for step in range(chips):
        origin = (chip + chips - step) % chips
        block = columns(origin, 1 - core)
        remote(tile, block, core_send.at[step], core_recv.at[step], peer(core=1 - core)).wait_recv()
    for origin in range(lines):
        block = slot(origin, 1 - side)
        remote(
            kv, block, side_send.at[origin], side_recv.at[origin], peer(side=1 - side)
        ).wait_recv()
    for copy in sends:
        copy.wait_send()
    for origin in range(lines):
        sideward(kv, origin).wait_send()

        @pl.when((line < lines - 1) & (origin <= line))
        def _():
            upward(kv, origin).wait_send()

        @pl.when((line > 0) & (origin >= line))
        def _():
            downward(kv, origin).wait_send()

    keep_kv.wait()
    keep_tile.wait()


def gather(kv, tile, rows, cols):
    lines, chips = rows // 2, cols // 2
    heads, height, width = tile.shape
    anywhere = pl.BlockSpec(memory_space=pl.ANY)
    dma = pltpu.SemaphoreType.DMA
    return pl.pallas_call(
        functools.partial(gather_kernel, lines, chips),
        out_shape=(
            jax.ShapeDtypeStruct((rows,) + kv.shape, kv.dtype),
            jax.ShapeDtypeStruct((heads, height, width * cols), tile.dtype),
        ),
        in_specs=[anywhere] * 2,
        out_specs=(anywhere, anywhere),
        scratch_shapes=[
            dma((2,)), dma((lines,)), dma((lines,)), dma((lines,)), dma((lines,)), dma((lines,)),
            dma((chips,)), dma((chips,)), dma((chips,)), dma((chips,)),
        ],
        compiler_params=pltpu.CompilerParams(
            collective_id=0, has_side_effects=True, vmem_limit_bytes=48 * 2**20
        ),
    )(kv, tile)


def reduce_kernel(
    lines, chips, dkv, ds, kv_sum, ds_sum,
    side_in, line_out, up_in, down_in, core_in, chip_out, chip_in,
    side_send, side_recv, line_send, up_recv, down_recv,
    core_send, core_recv, chip_send, chip_recv,
):
    line, side, chip, core = place()
    heads, height, width = ds_sum.shape
    depth = kv_sum.shape[0]
    greet(lines, chips)

    def columns(which_chip, which_core):
        start = pl.multiple_of((which_chip * 2 + which_core) * width, width)
        return pl.ds(start, width)

    sends = []
    for step in [*range(1, chips), 0]:
        copy = remote(
            ds.at[:, :, columns((chip + step) % chips, 1 - core)], core_in.at[step],
            core_send.at[step], core_recv.at[step], peer(core=1 - core),
        )
        copy.start()
        sends.append(copy)
    order = []
    for step in range(lines):
        for item in (lines - 1 - step, step):
            if item not in order:
                order.append(item)
    for item in order:
        copy = remote(
            dkv.at[item * 2 + 1 - side], side_in.at[item], side_send.at[item],
            side_recv.at[item], peer(side=1 - side),
        )
        copy.start()
        sends.append(copy)
    for step in range(1, chips):
        other = (chip + step) % chips
        sends[step - 1].wait_recv()

        @pl.loop(0, heads)
        def _(head):
            mine = ds[head, :, columns(other, core)].astype(jnp.float32)
            total = mine + core_in[step, head].astype(jnp.float32)
            chip_out[step, head] = total.astype(chip_out.dtype)

        copy = remote(
            chip_out.at[step], chip_in.at[step], chip_send.at[step], chip_recv.at[step],
            peer(chip=other),
        )
        copy.start()
        sends.append(copy)

    chunk = 16

    def pieces(write):
        @pl.loop(0, depth // chunk)
        def _(piece):
            write(pl.ds(pl.multiple_of(piece * chunk, chunk), chunk))

    def pair(target, part):
        mine = dkv[target * 2 + side, part, :].astype(jnp.float32)
        return mine + side_in[target, part, :].astype(jnp.float32)

    def side_wait(target):
        remote(
            dkv.at[0], side_in.at[target], side_send.at[target], side_recv.at[target],
            peer(side=1 - side),
        ).wait_recv()

    def upward(target):
        return remote(
            line_out.at[target], up_in.at[target], line_send.at[target], up_recv.at[target],
            peer(line=jnp.minimum(line + 1, lines - 1)),
        )

    def downward(target):
        return remote(
            line_out.at[target], down_in.at[target], line_send.at[target], down_recv.at[target],
            peer(line=jnp.maximum(line - 1, 0)),
        )

    def pass_on(target, make, arrived, first):
        side_wait(target)

        @pl.when(first)
        def _():
            def write(part):
                line_out[target, part, :] = pair(target, part).astype(line_out.dtype)

            pieces(write)

        @pl.when(jnp.logical_not(first))
        def _():
            make(target).wait_recv()

            def write(part):
                total = pair(target, part) + arrived[target, part, :].astype(jnp.float32)
                line_out[target, part, :] = total.astype(line_out.dtype)

            pieces(write)

        make(target).start()

    for step in range(lines - 1):
        top = lines - 1 - step

        @pl.when(line < top)
        def _():
            pass_on(top, upward, up_in, line == 0)

        @pl.when(line > step)
        def _():
            pass_on(step, downward, down_in, line == lines - 1)

    side_wait(line)

    def write_pair(part):
        kv_sum[part, :] = pair(line, part)

    pieces(write_pair)

    @pl.when(line > 0)
    def _():
        upward(line).wait_recv()

        def write(part):
            kv_sum[part, :] += up_in[line, part, :].astype(jnp.float32)

        pieces(write)

    @pl.when(line < lines - 1)
    def _():
        downward(line).wait_recv()

        def write(part):
            kv_sum[part, :] += down_in[line, part, :].astype(jnp.float32)

        pieces(write)

    sends[chips - 1].wait_recv()
    for step in range(1, chips):
        remote(
            chip_out.at[step], chip_in.at[step], chip_send.at[step], chip_recv.at[step],
            peer(core=1 - core),
        ).wait_recv()

    @pl.loop(0, heads)
    def _(head):
        total = ds[head, :, columns(chip, core)].astype(jnp.float32)
        total += core_in[0, head].astype(jnp.float32)
        for step in range(1, chips):
            total += chip_in[step, head].astype(jnp.float32)
        ds_sum[head] = total.astype(ds_sum.dtype)

    for copy in sends:
        copy.wait_send()
    for target in range(lines):
        @pl.when(line != target)
        def _():
            upward(target).wait_send()


def reduce(dkv, ds, rows, cols):
    lines, chips = rows // 2, cols // 2
    heads, height, width = ds.shape
    width //= cols
    depth, wide = dkv.shape[0] // rows, dkv.shape[1]
    inside = pl.BlockSpec(memory_space=pltpu.VMEM)
    dma = pltpu.SemaphoreType.DMA
    half = jnp.bfloat16
    return pl.pallas_call(
        functools.partial(reduce_kernel, lines, chips),
        out_shape=(
            jax.ShapeDtypeStruct((depth, wide), jnp.float32),
            jax.ShapeDtypeStruct((heads, height, width), jnp.float32),
        ),
        in_specs=[inside] * 2,
        out_specs=(inside, inside),
        scratch_shapes=[
            *[pltpu.VMEM((lines, depth, wide), half)] * 4,
            *[pltpu.VMEM((chips, heads, height, width), half)] * 3,
            *[dma((lines,))] * 5,
            *[dma((chips,))] * 4,
        ],
        compiler_params=pltpu.CompilerParams(
            collective_id=1, has_side_effects=True, vmem_limit_bytes=52 * 2**20
        ),
    )(dkv.reshape(rows, depth, wide), ds)


def lane_mean(values, ones):
    high = values.astype(jnp.bfloat16)
    low = (values - high.astype(jnp.float32)).astype(jnp.bfloat16)
    return jnp.dot(
        jnp.concatenate([high, low], axis=1), ones, preferred_element_type=jnp.float32
    )


def pair_standard(feats, centre, ones):
    centred = jnp.dot(feats, centre, preferred_element_type=jnp.float32)
    inv_std = lax.rsqrt(lane_mean(centred * centred, ones) + epsilon)
    return centred * inv_std, inv_std


def pair_forward_kernel(feats, centre, ones, gain, weights, out):
    total = None
    for item in range(feats.shape[0]):
        standard, _ = pair_standard(feats[item], centre[...], ones[...])
        normed = (standard * gain[...]).astype(jnp.bfloat16)
        part = jnp.dot(normed, weights[item], preferred_element_type=jnp.float32)
        total = part if total is None else total + part
    out[...] = total.T.reshape(out.shape).astype(jnp.bfloat16)


def pair_backward_kernel(feats, centre, ones, bias_grad, high_weights, low_weights, out):
    block, heads, width = bias_grad.shape
    grad = bias_grad[...].reshape(block * heads, width).T
    high = grad.astype(jnp.bfloat16)
    low = (grad - high.astype(jnp.float32)).astype(jnp.bfloat16)
    parts = jnp.concatenate([high, low], axis=1)
    for item in range(block):
        standard, inv_std = pair_standard(feats[item], centre[...], ones[...])
        scaled = jnp.dot(parts, high_weights[item], preferred_element_type=jnp.float32)
        scaled += jnp.dot(parts, low_weights[item], preferred_element_type=jnp.float32)
        cross_mean = lane_mean(scaled * standard, ones[...])
        out[item] = ((scaled - standard * cross_mean) * inv_std).astype(jnp.bfloat16)


def pair_call(kernel, pair_feats, extra, extra_specs, out_shape, block):
    rows, width, channels = pair_feats.shape
    eye = jnp.eye(channels, dtype=jnp.float32)
    centre = (eye - 1.0 / channels).astype(jnp.bfloat16)
    ones = jnp.full((2 * channels, channels), 1.0 / channels, jnp.bfloat16)
    whole = lambda shape: pl.BlockSpec(shape, lambda step: (0,) * len(shape))
    tiled = lambda shape: pl.BlockSpec((block,) + shape[1:], lambda step: (step, 0, 0))
    return pl.pallas_call(
        kernel,
        grid=(rows // block,),
        out_shape=jax.ShapeDtypeStruct(out_shape, jnp.bfloat16),
        in_specs=[
            tiled(pair_feats.shape), whole(centre.shape), whole(ones.shape),
            *[(tiled if spec else whole)(item.shape) for item, spec in zip(extra, extra_specs)],
        ],
        out_specs=tiled(out_shape),
        compiler_params=pltpu.CompilerParams(vmem_limit_bytes=32 * 2**20),
    )(pair_feats, centre, ones, *extra)


def spread(matrix, block, axis):
    picks = jnp.eye(block, dtype=matrix.dtype)
    if axis == 1:
        full = picks[:, None, :, None] * matrix[None, :, None, :]
        return full.reshape(block, matrix.shape[0], block * matrix.shape[1])
    full = picks[:, :, None, None] * matrix[None, None]
    full = full.reshape(block, block * matrix.shape[0], matrix.shape[1])
    return jnp.concatenate([full, full], axis=1)


def pair_forward(pair_feats, pair_gain, w_pair):
    rows, width, channels = pair_feats.shape
    heads = w_pair.shape[1]
    block = 128 // heads
    return pair_call(
        pair_forward_kernel, pair_feats, (pair_gain[None], spread(w_pair, block, 1)),
        (False, False), (rows, heads, width), block,
    )


def pair_backward(pair_feats, pair_gain, w_pair, bias_grad):
    block = 128 // w_pair.shape[1]
    scaled = w_pair.astype(jnp.float32).T * pair_gain
    scaled = scaled - jnp.mean(scaled, axis=1, keepdims=True)
    high = lax.reduce_precision(scaled, 8, 7)
    low = (scaled - high).astype(jnp.bfloat16)
    high = high.astype(jnp.bfloat16)
    return pair_call(
        pair_backward_kernel, pair_feats,
        (jnp.transpose(bias_grad, (1, 0, 2)), spread(high, block, 0), spread(low, block, 0)),
        (True, False, False), pair_feats.shape, block,
    )


def body(
    rows,
    cols,
    token_acts,
    pair_feats,
    pair_mask,
    norm_gain,
    norm_shift,
    w_query,
    query_bias,
    w_key,
    w_value,
    w_gate,
    w_out,
    pair_gain,
    w_pair,
    grad_out,
):
    row_count = token_acts.shape[1]
    model_width = token_acts.shape[2]
    col_count = pair_feats.shape[1]
    head_count = w_pair.shape[1]
    head_size = model_width // head_count
    score_scale = 1.0 / math.sqrt(head_size)
    row_start = lax.axis_index("row") * row_count
    col_start = lax.axis_index("col") * col_count
    pair_bias = jnp.transpose(pair_forward(pair_feats, pair_gain, w_pair), (1, 0, 2))
    row_index = row_start + lax.broadcasted_iota(jnp.int32, (row_count, col_count), 0)
    col_index = col_start + lax.broadcasted_iota(jnp.int32, (row_count, col_count), 1)
    allowed = (pair_mask == 1) | (row_index == col_index)
    biased = jnp.where(allowed[None], pair_bias, jnp.bfloat16(-1000000000.0))
    standard, inv_std = normalize(token_acts[0].astype(jnp.float32))
    normed = (standard * norm_gain + norm_shift).astype(jnp.bfloat16)
    query = (jnp.dot(normed, w_query, preferred_element_type=jnp.float32) + query_bias).astype(
        jnp.bfloat16
    )
    gate_open = jax.nn.sigmoid(jnp.dot(normed, w_gate, preferred_element_type=jnp.float32))
    own_keys = jnp.dot(normed, w_key, preferred_element_type=jnp.float32).astype(jnp.bfloat16)
    own_values = jnp.dot(normed, w_value, preferred_element_type=jnp.float32).astype(jnp.bfloat16)
    both, bias_full = gather(jnp.concatenate([own_keys, own_values], axis=1), biased, rows, cols)
    both = both.reshape(rows * row_count, 2 * model_width)
    all_keys, all_values = both[:, :model_width], both[:, model_width:]
    key_count = all_keys.shape[0]
    query_heads = query.reshape(row_count, head_count, head_size)
    key_heads = all_keys.reshape(key_count, head_count, head_size)
    value_heads = all_values.reshape(key_count, head_count, head_size)
    scores = jnp.einsum(
        "ihe,jhe->hij", query_heads, key_heads, preferred_element_type=jnp.float32
    ) * score_scale + bias_full.astype(jnp.float32)
    attn_probs = jax.nn.softmax(scores, axis=-1)
    probs_b = attn_probs.astype(jnp.bfloat16)
    attended = jnp.einsum(
        "hij,jhe->ihe", probs_b, value_heads, preferred_element_type=jnp.float32
    ).reshape(row_count, model_width)
    gated_out = (gate_open * attended).astype(jnp.bfloat16)
    block_out = jnp.dot(gated_out, w_out, preferred_element_type=jnp.float32).astype(jnp.bfloat16)
    d_gated = jnp.einsum("io,do->id", grad_out[0], w_out, preferred_element_type=jnp.float32)
    d_att = (d_gated * gate_open).astype(jnp.bfloat16)
    d_gate_pre = d_gated * attended * gate_open * (1.0 - gate_open)
    att_heads = d_att.reshape(row_count, head_count, head_size)
    d_probs = jnp.einsum("ihe,jhe->hij", att_heads, value_heads, preferred_element_type=jnp.float32)
    row_delta = jnp.sum(attn_probs * d_probs, axis=-1, keepdims=True)
    d_scores = attn_probs * (d_probs - row_delta)
    ds_b = d_scores.astype(jnp.bfloat16)
    d_query = (
        jnp.einsum("hij,jhe->ihe", ds_b, key_heads, preferred_element_type=jnp.float32)
        * score_scale
    ).reshape(row_count, model_width)
    d_keys = (
        jnp.einsum("hij,ihe->jhe", ds_b, query_heads, preferred_element_type=jnp.float32)
        * score_scale
    ).reshape(key_count, model_width)
    d_values = jnp.einsum(
        "hij,ihe->jhe", probs_b, att_heads, preferred_element_type=jnp.float32
    ).reshape(key_count, model_width)
    near_part = back_project(d_query, w_query) + back_project(d_gate_pre, w_gate)
    summed, bias_grad = reduce(
        jnp.concatenate([d_keys, d_values], axis=1).astype(jnp.bfloat16), ds_b, rows, cols
    )
    key_grad, value_grad = summed[:, :model_width], summed[:, model_width:]
    far_part = back_project(key_grad, w_key) + back_project(value_grad, w_value)
    d_normed = near_part + far_part
    grad_acts = norm_backward(standard, inv_std, norm_gain, d_normed).astype(jnp.bfloat16)
    grad_pair = pair_backward(pair_feats, pair_gain, w_pair, bias_grad)
    return (block_out[None], grad_acts[None], grad_pair)


def solution(mesh):
    placed = (
        P("col", "row", None),
        P("row", "col", None),
        P("row", "col"),
        P(),
        P(),
        P(),
        P(),
        P(),
        P(),
        P(),
        P(),
        P(),
        P(),
        P("col", "row", None),
    )
    return jax.shard_map(
        functools.partial(body, mesh.shape["row"], mesh.shape["col"]),
        mesh=mesh,
        in_specs=placed,
        out_specs=(P("col", "row", None), P("col", "row", None), P("row", "col", None)),
        check_vma=False,
    )
```

```python
import functools
import math

import jax
import jax.numpy as jnp
from jax import lax
from jax.experimental import pallas as pl
from jax.experimental.pallas import tpu as pltpu
from jax.sharding import PartitionSpec as P

epsilon = 1e-05
highest = lax.Precision.HIGHEST


def normalize(inputs):
    row_mean = jnp.mean(inputs, axis=-1, keepdims=True)
    centred = inputs - row_mean
    variance = jnp.mean(centred * centred, axis=-1, keepdims=True)
    inv_std = lax.rsqrt(variance + epsilon)
    return (centred * inv_std, inv_std)


def norm_backward(standard, inv_std, gain_vec, upstream):
    scaled = upstream * gain_vec
    grad_mean = jnp.mean(scaled, axis=-1, keepdims=True)
    cross_mean = jnp.mean(scaled * standard, axis=-1, keepdims=True)
    return (scaled - grad_mean - standard * cross_mean) * inv_std


def back_project(upstream, matrix):
    return jnp.einsum("io,do->id", upstream, matrix.astype(jnp.float32), precision=highest)


def place():
    row, col = lax.axis_index("row"), lax.axis_index("col")
    return row // 2, row % 2, col // 2, col % 2


def peer(line=None, side=None, chip=None, core=None):
    own = place()
    line, side, chip, core = (
        mine if given is None else given for mine, given in zip(own, (line, side, chip, core))
    )
    return (line * 2 + side, chip * 2 + core)


def remote(source, target, send_sem, recv_sem, device):
    return pltpu.make_async_remote_copy(
        src_ref=source,
        dst_ref=target,
        send_sem=send_sem,
        recv_sem=recv_sem,
        device_id=device,
        device_id_type=pl.DeviceIdType.MESH,
    )


def greet(lines, chips):
    line, side, chip, core = place()
    barrier = pltpu.get_barrier_semaphore()
    others = [peer(side=1 - side), peer(core=1 - core)]
    others += [peer(line=(line + 1) % lines), peer(line=(line + lines - 1) % lines)]
    others += [peer(chip=(chip + step) % chips) for step in range(1, chips)]
    for other in others:
        pl.semaphore_signal(barrier, inc=1, device_id=other, device_id_type=pl.DeviceIdType.MESH)
    pl.semaphore_wait(barrier, len(others))


def gather_kernel(
    lines, chips, kv, tile, kv_all, bias_all,
    local_sem, up_send, down_send, side_send, line_recv, side_recv,
    chip_send, chip_recv, core_send, core_recv,
):
    line, side, chip, core = place()
    width = tile.shape[2]
    greet(lines, chips)

    def slot(which_line, which_side):
        return kv_all.at[which_line * 2 + which_side]

    def columns(which_chip, which_core):
        start = pl.multiple_of((which_chip * 2 + which_core) * width, width)
        return bias_all.at[:, :, pl.ds(start, width)]

    sends = []
    for step in range(1, chips):
        sends.append(remote(
            tile, columns(chip, core), chip_send.at[step], chip_recv.at[step],
            peer(chip=(chip + step) % chips),
        ))
    sends.append(remote(
        tile, columns(chip, core), core_send.at[0], core_recv.at[0], peer(core=1 - core)
    ))
    for copy in sends:
        copy.start()

    def upward(source, origin):
        return remote(
            source, slot(origin, side), up_send.at[origin], line_recv.at[origin],
            peer(line=jnp.minimum(line + 1, lines - 1)),
        )

    def downward(source, origin):
        return remote(
            source, slot(origin, side), down_send.at[origin], line_recv.at[origin],
            peer(line=jnp.maximum(line - 1, 0)),
        )

    def sideward(source, origin):
        return remote(
            source, slot(origin, side), side_send.at[origin], side_recv.at[origin],
            peer(side=1 - side),
        )

    @pl.when(line < lines - 1)
    def _():
        upward(kv, line).start()

    @pl.when(line > 0)
    def _():
        downward(kv, line).start()

    sideward(kv, line).start()
    keep_kv = pltpu.make_async_copy(kv, slot(line, side), local_sem.at[0])
    keep_tile = pltpu.make_async_copy(tile, columns(chip, core), local_sem.at[1])
    keep_kv.start()
    keep_tile.start()

    for step in range(1, lines):
        @pl.when(line - step >= 0)
        def _():
            origin = line - step
            upward(slot(origin, side), origin).wait_recv()

            @pl.when(line < lines - 1)
            def _():
                upward(slot(origin, side), origin).start()

            sideward(slot(origin, side), origin).start()

        @pl.when(line + step < lines)
        def _():
            origin = line + step
            downward(slot(origin, side), origin).wait_recv()

            @pl.when(line > 0)
            def _():
                downward(slot(origin, side), origin).start()

            sideward(slot(origin, side), origin).start()

    for step in range(1, chips):
        origin = (chip + chips - step) % chips
        block = columns(origin, core)
        remote(tile, block, chip_send.at[step], chip_recv.at[step], peer(core=1 - core)).wait_recv()
        copy = remote(block, block, core_send.at[step], core_recv.at[step], peer(core=1 - core))
        copy.start()
        sends.append(copy)
    for step in range(chips):
        origin = (chip + chips - step) % chips
        block = columns(origin, 1 - core)
        remote(tile, block, core_send.at[step], core_recv.at[step], peer(core=1 - core)).wait_recv()
    for origin in range(lines):
        block = slot(origin, 1 - side)
        remote(
            kv, block, side_send.at[origin], side_recv.at[origin], peer(side=1 - side)
        ).wait_recv()
    for copy in sends:
        copy.wait_send()
    for origin in range(lines):
        sideward(kv, origin).wait_send()

        @pl.when((line < lines - 1) & (origin <= line))
        def _():
            upward(kv, origin).wait_send()

        @pl.when((line > 0) & (origin >= line))
        def _():
            downward(kv, origin).wait_send()

    keep_kv.wait()
    keep_tile.wait()


def gather(kv, tile, rows, cols):
    lines, chips = rows // 2, cols // 2
    heads, height, width = tile.shape
    anywhere = pl.BlockSpec(memory_space=pl.ANY)
    dma = pltpu.SemaphoreType.DMA
    return pl.pallas_call(
        functools.partial(gather_kernel, lines, chips),
        out_shape=(
            jax.ShapeDtypeStruct((rows,) + kv.shape, kv.dtype),
            jax.ShapeDtypeStruct((heads, height, width * cols), tile.dtype),
        ),
        in_specs=[anywhere] * 2,
        out_specs=(anywhere, anywhere),
        scratch_shapes=[
            dma((2,)), dma((lines,)), dma((lines,)), dma((lines,)), dma((lines,)), dma((lines,)),
            dma((chips,)), dma((chips,)), dma((chips,)), dma((chips,)),
        ],
        compiler_params=pltpu.CompilerParams(
            collective_id=0, has_side_effects=True, vmem_limit_bytes=48 * 2**20
        ),
    )(kv, tile)


def reduce_kernel(
    lines, chips, dkv, ds, kv_sum, ds_sum,
    side_in, line_out, up_in, down_in, core_in, chip_out, chip_in,
    side_send, side_recv, line_send, up_recv, down_recv,
    core_send, core_recv, chip_send, chip_recv,
):
    line, side, chip, core = place()
    heads, height, width = ds_sum.shape
    depth = kv_sum.shape[0]
    greet(lines, chips)

    def columns(which_chip, which_core):
        start = pl.multiple_of((which_chip * 2 + which_core) * width, width)
        return pl.ds(start, width)

    sends = []
    for step in [*range(1, chips), 0]:
        copy = remote(
            ds.at[:, :, columns((chip + step) % chips, 1 - core)], core_in.at[step],
            core_send.at[step], core_recv.at[step], peer(core=1 - core),
        )
        copy.start()
        sends.append(copy)
    order = []
    for step in range(lines):
        for item in (lines - 1 - step, step):
            if item not in order:
                order.append(item)
    for item in order:
        copy = remote(
            dkv.at[item * 2 + 1 - side], side_in.at[item], side_send.at[item],
            side_recv.at[item], peer(side=1 - side),
        )
        copy.start()
        sends.append(copy)
    for step in range(1, chips):
        other = (chip + step) % chips
        sends[step - 1].wait_recv()

        @pl.loop(0, heads)
        def _(head):
            mine = ds[head, :, columns(other, core)].astype(jnp.float32)
            total = mine + core_in[step, head].astype(jnp.float32)
            chip_out[step, head] = total.astype(chip_out.dtype)

        copy = remote(
            chip_out.at[step], chip_in.at[step], chip_send.at[step], chip_recv.at[step],
            peer(chip=other),
        )
        copy.start()
        sends.append(copy)

    chunk = 16

    def pieces(write):
        @pl.loop(0, depth // chunk)
        def _(piece):
            write(pl.ds(pl.multiple_of(piece * chunk, chunk), chunk))

    def pair(target, part):
        mine = dkv[target * 2 + side, part, :].astype(jnp.float32)
        return mine + side_in[target, part, :].astype(jnp.float32)

    def side_wait(target):
        remote(
            dkv.at[0], side_in.at[target], side_send.at[target], side_recv.at[target],
            peer(side=1 - side),
        ).wait_recv()

    def upward(target):
        return remote(
            line_out.at[target], up_in.at[target], line_send.at[target], up_recv.at[target],
            peer(line=jnp.minimum(line + 1, lines - 1)),
        )

    def downward(target):
        return remote(
            line_out.at[target], down_in.at[target], line_send.at[target], down_recv.at[target],
            peer(line=jnp.maximum(line - 1, 0)),
        )

    def pass_on(target, make, arrived, first):
        side_wait(target)

        @pl.when(first)
        def _():
            def write(part):
                line_out[target, part, :] = pair(target, part).astype(line_out.dtype)

            pieces(write)

        @pl.when(jnp.logical_not(first))
        def _():
            make(target).wait_recv()

            def write(part):
                total = pair(target, part) + arrived[target, part, :].astype(jnp.float32)
                line_out[target, part, :] = total.astype(line_out.dtype)

            pieces(write)

        make(target).start()

    for step in range(lines - 1):
        top = lines - 1 - step

        @pl.when(line < top)
        def _():
            pass_on(top, upward, up_in, line == 0)

        @pl.when(line > step)
        def _():
            pass_on(step, downward, down_in, line == lines - 1)

    side_wait(line)

    def write_pair(part):
        kv_sum[part, :] = pair(line, part)

    pieces(write_pair)

    @pl.when(line > 0)
    def _():
        upward(line).wait_recv()

        def write(part):
            kv_sum[part, :] += up_in[line, part, :].astype(jnp.float32)

        pieces(write)

    @pl.when(line < lines - 1)
    def _():
        downward(line).wait_recv()

        def write(part):
            kv_sum[part, :] += down_in[line, part, :].astype(jnp.float32)

        pieces(write)

    sends[chips - 1].wait_recv()
    for step in range(1, chips):
        remote(
            chip_out.at[step], chip_in.at[step], chip_send.at[step], chip_recv.at[step],
            peer(core=1 - core),
        ).wait_recv()

    @pl.loop(0, heads)
    def _(head):
        total = ds[head, :, columns(chip, core)].astype(jnp.float32)
        total += core_in[0, head].astype(jnp.float32)
        for step in range(1, chips):
            total += chip_in[step, head].astype(jnp.float32)
        ds_sum[head] = total.astype(ds_sum.dtype)

    for copy in sends:
        copy.wait_send()
    for target in range(lines):
        @pl.when(line != target)
        def _():
            upward(target).wait_send()


def reduce(dkv, ds, rows, cols):
    lines, chips = rows // 2, cols // 2
    heads, height, width = ds.shape
    width //= cols
    depth, wide = dkv.shape[0] // rows, dkv.shape[1]
    inside = pl.BlockSpec(memory_space=pltpu.VMEM)
    dma = pltpu.SemaphoreType.DMA
    half = jnp.bfloat16
    return pl.pallas_call(
        functools.partial(reduce_kernel, lines, chips),
        out_shape=(
            jax.ShapeDtypeStruct((depth, wide), jnp.float32),
            jax.ShapeDtypeStruct((heads, height, width), jnp.float32),
        ),
        in_specs=[inside] * 2,
        out_specs=(inside, inside),
        scratch_shapes=[
            *[pltpu.VMEM((lines, depth, wide), half)] * 4,
            *[pltpu.VMEM((chips, heads, height, width), half)] * 3,
            *[dma((lines,))] * 5,
            *[dma((chips,))] * 4,
        ],
        compiler_params=pltpu.CompilerParams(
            collective_id=1, has_side_effects=True, vmem_limit_bytes=52 * 2**20
        ),
    )(dkv.reshape(rows, depth, wide), ds)


def lane_mean(values, ones):
    high = values.astype(jnp.bfloat16)
    low = (values - high.astype(jnp.float32)).astype(jnp.bfloat16)
    return jnp.dot(
        jnp.concatenate([high, low], axis=1), ones, preferred_element_type=jnp.float32
    )


def pair_standard(feats, centre, ones):
    centred = jnp.dot(feats, centre, preferred_element_type=jnp.float32)
    inv_std = lax.rsqrt(lane_mean(centred * centred, ones) + epsilon)
    return centred * inv_std, inv_std


def pair_forward_kernel(feats, centre, ones, gain, weights, out):
    total = None
    for item in range(feats.shape[0]):
        standard, _ = pair_standard(feats[item], centre[...], ones[...])
        normed = (standard * gain[...]).astype(jnp.bfloat16)
        part = jnp.dot(normed, weights[item], preferred_element_type=jnp.float32)
        total = part if total is None else total + part
    out[...] = total.T.reshape(out.shape).astype(jnp.bfloat16)


def pair_backward_kernel(feats, centre, ones, bias_grad, weights, out):
    for item in range(feats.shape[0]):
        standard, inv_std = pair_standard(feats[item], centre[...], ones[...])
        grad = bias_grad[item]
        high = grad.astype(jnp.bfloat16).astype(jnp.float32)
        low = grad - high
        parts = jnp.concatenate([high, low, high, low], axis=0).T.astype(jnp.bfloat16)
        scaled = jnp.dot(parts, weights[...], preferred_element_type=jnp.float32)
        cross_mean = lane_mean(scaled * standard, ones[...])
        out[item] = ((scaled - standard * cross_mean) * inv_std).astype(jnp.bfloat16)


def pair_call(kernel, pair_feats, extra, extra_specs, out_shape, block):
    rows, width, channels = pair_feats.shape
    eye = jnp.eye(channels, dtype=jnp.float32)
    centre = (eye - 1.0 / channels).astype(jnp.bfloat16)
    ones = jnp.full((2 * channels, channels), 1.0 / channels, jnp.bfloat16)
    whole = lambda shape: pl.BlockSpec(shape, lambda step: (0,) * len(shape))
    tiled = lambda shape: pl.BlockSpec((block,) + shape[1:], lambda step: (step, 0, 0))
    return pl.pallas_call(
        kernel,
        grid=(rows // block,),
        out_shape=jax.ShapeDtypeStruct(out_shape, jnp.bfloat16),
        in_specs=[
            tiled(pair_feats.shape), whole(centre.shape), whole(ones.shape),
            *[(tiled if spec else whole)(item.shape) for item, spec in zip(extra, extra_specs)],
        ],
        out_specs=tiled(out_shape),
        compiler_params=pltpu.CompilerParams(vmem_limit_bytes=32 * 2**20),
    )(pair_feats, centre, ones, *extra)


def spread(matrix, block):
    picks = jnp.eye(block, dtype=matrix.dtype)
    full = picks[:, None, :, None] * matrix[None, :, None, :]
    return full.reshape(block, matrix.shape[0], block * matrix.shape[1])


def pair_forward(pair_feats, pair_gain, w_pair):
    rows, width, channels = pair_feats.shape
    heads = w_pair.shape[1]
    block = 128 // heads
    return pair_call(
        pair_forward_kernel, pair_feats, (pair_gain[None], spread(w_pair, block)),
        (False, False), (rows, heads, width), block,
    )


def pair_backward(pair_feats, pair_gain, w_pair, bias_grad):
    scaled = w_pair.astype(jnp.float32).T * pair_gain
    scaled = scaled - jnp.mean(scaled, axis=1, keepdims=True)
    high = lax.reduce_precision(scaled, 8, 7)
    low = scaled - high
    weights = jnp.concatenate([high, high, low, low], axis=0).astype(jnp.bfloat16)
    return pair_call(
        pair_backward_kernel, pair_feats, (jnp.transpose(bias_grad, (1, 0, 2)), weights),
        (True, False), pair_feats.shape, 8,
    )


def body(
    rows,
    cols,
    token_acts,
    pair_feats,
    pair_mask,
    norm_gain,
    norm_shift,
    w_query,
    query_bias,
    w_key,
    w_value,
    w_gate,
    w_out,
    pair_gain,
    w_pair,
    grad_out,
):
    row_count = token_acts.shape[1]
    model_width = token_acts.shape[2]
    col_count = pair_feats.shape[1]
    head_count = w_pair.shape[1]
    head_size = model_width // head_count
    score_scale = 1.0 / math.sqrt(head_size)
    row_start = lax.axis_index("row") * row_count
    col_start = lax.axis_index("col") * col_count
    pair_bias = jnp.transpose(pair_forward(pair_feats, pair_gain, w_pair), (1, 0, 2))
    row_index = row_start + lax.broadcasted_iota(jnp.int32, (row_count, col_count), 0)
    col_index = col_start + lax.broadcasted_iota(jnp.int32, (row_count, col_count), 1)
    allowed = (pair_mask == 1) | (row_index == col_index)
    biased = jnp.where(allowed[None], pair_bias, jnp.bfloat16(-1000000000.0))
    standard, inv_std = normalize(token_acts[0].astype(jnp.float32))
    normed = (standard * norm_gain + norm_shift).astype(jnp.bfloat16)
    query = (jnp.dot(normed, w_query, preferred_element_type=jnp.float32) + query_bias).astype(
        jnp.bfloat16
    )
    gate_open = jax.nn.sigmoid(jnp.dot(normed, w_gate, preferred_element_type=jnp.float32))
    own_keys = jnp.dot(normed, w_key, preferred_element_type=jnp.float32).astype(jnp.bfloat16)
    own_values = jnp.dot(normed, w_value, preferred_element_type=jnp.float32).astype(jnp.bfloat16)
    both, bias_full = gather(jnp.concatenate([own_keys, own_values], axis=1), biased, rows, cols)
    both = both.reshape(rows * row_count, 2 * model_width)
    all_keys, all_values = both[:, :model_width], both[:, model_width:]
    key_count = all_keys.shape[0]
    query_heads = query.reshape(row_count, head_count, head_size)
    key_heads = all_keys.reshape(key_count, head_count, head_size)
    value_heads = all_values.reshape(key_count, head_count, head_size)
    scores = jnp.einsum(
        "ihe,jhe->hij", query_heads, key_heads, preferred_element_type=jnp.float32
    ) * score_scale + bias_full.astype(jnp.float32)
    attn_probs = jax.nn.softmax(scores, axis=-1)
    probs_b = attn_probs.astype(jnp.bfloat16)
    attended = jnp.einsum(
        "hij,jhe->ihe", probs_b, value_heads, preferred_element_type=jnp.float32
    ).reshape(row_count, model_width)
    gated_out = (gate_open * attended).astype(jnp.bfloat16)
    block_out = jnp.dot(gated_out, w_out, preferred_element_type=jnp.float32).astype(jnp.bfloat16)
    d_gated = jnp.einsum("io,do->id", grad_out[0], w_out, preferred_element_type=jnp.float32)
    d_att = (d_gated * gate_open).astype(jnp.bfloat16)
    d_gate_pre = d_gated * attended * gate_open * (1.0 - gate_open)
    att_heads = d_att.reshape(row_count, head_count, head_size)
    d_probs = jnp.einsum("ihe,jhe->hij", att_heads, value_heads, preferred_element_type=jnp.float32)
    row_delta = jnp.sum(attn_probs * d_probs, axis=-1, keepdims=True)
    d_scores = attn_probs * (d_probs - row_delta)
    ds_b = d_scores.astype(jnp.bfloat16)
    d_query = (
        jnp.einsum("hij,jhe->ihe", ds_b, key_heads, preferred_element_type=jnp.float32)
        * score_scale
    ).reshape(row_count, model_width)
    d_keys = (
        jnp.einsum("hij,ihe->jhe", ds_b, query_heads, preferred_element_type=jnp.float32)
        * score_scale
    ).reshape(key_count, model_width)
    d_values = jnp.einsum(
        "hij,ihe->jhe", probs_b, att_heads, preferred_element_type=jnp.float32
    ).reshape(key_count, model_width)
    near_part = back_project(d_query, w_query) + back_project(d_gate_pre, w_gate)
    summed, bias_grad = reduce(
        jnp.concatenate([d_keys, d_values], axis=1).astype(jnp.bfloat16), ds_b, rows, cols
    )
    key_grad, value_grad = summed[:, :model_width], summed[:, model_width:]
    far_part = back_project(key_grad, w_key) + back_project(value_grad, w_value)
    d_normed = near_part + far_part
    grad_acts = norm_backward(standard, inv_std, norm_gain, d_normed).astype(jnp.bfloat16)
    grad_pair = pair_backward(pair_feats, pair_gain, w_pair, bias_grad)
    return (block_out[None], grad_acts[None], grad_pair)


def solution(mesh):
    placed = (
        P("col", "row", None),
        P("row", "col", None),
        P("row", "col"),
        P(),
        P(),
        P(),
        P(),
        P(),
        P(),
        P(),
        P(),
        P(),
        P(),
        P("col", "row", None),
    )
    return jax.shard_map(
        functools.partial(body, mesh.shape["row"], mesh.shape["col"]),
        mesh=mesh,
        in_specs=placed,
        out_specs=(P("col", "row", None), P("col", "row", None), P("row", "col", None)),
        check_vma=False,
    )
```
